256 devices in a mesh: dp: 32 (over z, x), tensor: 8 (over y, core).
Axes of the slice: x: 4, y: 4, z: 8, core: 2. Of those that a mesh axis runs over, the one named last changes fastest.
Arguments:
- queries: bfloat16 [20480, 4096], P('dp', 'tensor'), may hold values from -6 to 6
- resp_kv: bfloat16 [20480, 2048], P('dp', 'tensor'), may hold values from -6 to 6
- prompt_kv: bfloat16 [512, 512, 2048], P('dp', None, 'tensor'), may hold values from -6 to 6
- prompt_len: int32 [512], replicated, may hold values from 128 to 512
- resp_len: int32 [512, 5], P('dp'), may hold values from 1 to 8
- dest: int32 [512], replicated, may hold values from 0 to 511, as said below
- wo: bfloat16 [4096, 8192], P('tensor'), may hold values from -0.09375 to 0.09375
- residual: bfloat16 [20480, 8192], P(('dp', 'tensor')), may hold values from -6 to 6
Outputs:
- hidden: bfloat16 [20480, 8192], P(('dp', 'tensor'))
The draws below stay inside these ranges and needn't reach their ends.
Inputs may be any that keep to these rules, and one draw needn't show every extreme that they name: dest is a permutation; the 16 prompts prefilled on one dp index go to 16 different dp indices (slot // 16), so every dp index receives exactly 16 prompts, from different indices.
All inputs are finite; a program needn't handle non-finite values.
Results may differ from the reference program's by a relative error of at most 0.007.
Values may be sent and summed in bfloat16 or wider, within the bound.
A program may use at most 128 MiB of HBM per device.

```python
import jax
import jax.numpy as jnp
from jax import lax

D = 8192
HEADS = 32
KV_HEADS = 8
HD = 128
RESP = 5
PLEN = 512
RLEN = 8
P_DEV = 16
NP = 512
ROWS = 20480
N_DP = 32


def draw_dest(key, part):
    key = jax.random.fold_in(key, 11)
    first, second = jax.random.split(key)
    ranks = jax.random.permutation(first, N_DP).astype(jnp.int32)
    ranks = ranks.at[1].set(-2).at[N_DP // 2].set(-1)
    offsets = jnp.argsort(ranks, stable=True)[:P_DEV]
    senders = jnp.arange(N_DP)[:, None]
    target = (senders + offsets[None, :]) % N_DP
    keys = jax.random.split(second, N_DP)
    orders = jax.vmap(lambda one: jax.random.permutation(one, P_DEV))(keys)
    within = orders[target, jnp.arange(P_DEV)[None, :]]
    return (target * P_DEV + within).reshape(-1).astype(jnp.int32)


def draw_queries(key, part):
    inner = jax.random.fold_in(key, 21)
    drawn = jax.random.truncated_normal(inner, -6.0, 6.0, (ROWS, HEADS * HD), jnp.float32)
    return drawn.astype(jnp.bfloat16)


def draw_prompt_kv(key, part):
    inner = jax.random.fold_in(key, 31)
    drawn = jax.random.truncated_normal(inner, -6.0, 6.0, (NP, PLEN, KV_HEADS * 2 * HD), jnp.float32)
    return drawn.astype(jnp.bfloat16)


def plant(values, key, low, top_value):
    extent = values.shape
    index_at = [jax.random.randint(jax.random.fold_in(key, axis), (), 0, extent[axis]) for axis in range(len(extent))]
    values = values.at[tuple(index_at)].set(low)
    longest = extent.index(max(extent))
    index_at[longest] = (index_at[longest] + 1) % extent[longest]
    return values.at[tuple(index_at)].set(top_value)


def level_of(key, shape, cuts, least, high):
    loudness = 1.0
    for axis_at, blocks in cuts:
        draws = jax.random.uniform(jax.random.fold_in(jax.random.fold_in(key, 6), axis_at), (blocks,), jnp.float32, least / len(cuts), high / len(cuts))
        loudness = loudness * jnp.repeat(jnp.exp(draws), shape[axis_at] // blocks).reshape((-1,) + (1,) * (len(shape) - 1 - axis_at))
    return loudness


def gaussian(own_key, dims, width, most, pieces=(), kind=jnp.bfloat16):
    values = width * jax.random.normal(own_key, dims, jnp.float32)
    if pieces:
        values = values * level_of(own_key, dims, pieces, -0.22, 0.18)
    return jnp.clip(values, -most, most).astype(kind)


def setup_inputs(seed: int = 0) -> dict:
    seeds = jax.random.split(jax.random.key(seed), 9)
    return {
        "queries": draw_queries(jax.random.fold_in(seeds[8], 71), 0),
        "resp_kv": gaussian(seeds[1], (ROWS, KV_HEADS * 2 * HD), 1.0, 6.0, ((0, 32), (1, 8))),
        "prompt_kv": draw_prompt_kv(jax.random.fold_in(seeds[8], 71), 0),
        "prompt_len": plant(jax.random.randint(seeds[3], (NP,), PLEN // 4, PLEN + 1), jax.random.fold_in(seeds[3], 1), PLEN // 4, PLEN).astype(jnp.int32),
        "resp_len": plant(jax.random.randint(seeds[4], (NP, RESP), 1, RLEN + 1), jax.random.fold_in(seeds[4], 1), 1, RLEN).astype(jnp.int32),
        "dest": draw_dest(jax.random.fold_in(seeds[8], 71), 0),
        "wo": gaussian(seeds[6], (HEADS * HD, D), (HEADS * HD) ** -0.5, 0.09375, ((0, 8),)),
        "residual": gaussian(seeds[7], (ROWS, D), 1.0, 6.0, ((0, 256),)),
    }


def reference(queries, resp_kv, prompt_kv, prompt_len, resp_len, dest, wo, residual):
    count = prompt_kv.shape[0]
    inverse = jnp.zeros((count,), jnp.int32).at[dest].set(jnp.arange(count, dtype=jnp.int32))
    group = HEADS // KV_HEADS
    rows = RESP * RLEN
    scale = HD ** -0.5

    def one_slot(slot):
        prompt = inverse[slot]
        block = lax.dynamic_index_in_dim(prompt_kv, prompt, 0, keepdims=False)
        block = block.reshape(PLEN, KV_HEADS, 2, HD).astype(jnp.float32)
        live = prompt_len[prompt]
        start = (slot * rows).astype(jnp.int32)
        query = lax.dynamic_slice_in_dim(queries, start, rows, 0)
        query = query.reshape(RESP, RLEN, KV_HEADS, group, HD).astype(jnp.float32)
        own = lax.dynamic_slice_in_dim(resp_kv, start, rows, 0)
        own = own.reshape(RESP, RLEN, KV_HEADS, 2, HD).astype(jnp.float32)
        score_p = jnp.einsum("rthgd,shd->rthgs", query, block[:, :, 0]) * scale
        score_r = jnp.einsum("rthgd,ruhd->rthgu", query, own[:, :, :, 0]) * scale
        pmask = (jnp.arange(PLEN) < live)[None, None, None, None, :]
        causal = (jnp.arange(RLEN)[:, None] >= jnp.arange(RLEN)[None, :])[None, :, None, None, :]
        score_p = jnp.where(pmask, score_p, -1e30)
        score_r = jnp.where(causal, score_r, -1e30)
        top = jnp.maximum(jnp.max(score_p, axis=-1), jnp.max(score_r, axis=-1))[..., None]
        exp_p = jnp.exp(score_p - top)
        exp_r = jnp.exp(score_r - top)
        total = jnp.sum(exp_p, axis=-1, keepdims=True) + jnp.sum(exp_r, axis=-1, keepdims=True)
        weight_p = (exp_p / total).astype(jnp.bfloat16).astype(jnp.float32)
        weight_r = (exp_r / total).astype(jnp.bfloat16).astype(jnp.float32)
        out = jnp.einsum("rthgs,shd->rthgd", weight_p, block[:, :, 1])
        out = out + jnp.einsum("rthgu,ruhd->rthgd", weight_r, own[:, :, :, 1])
        valid = jnp.arange(RLEN)[None, :] < resp_len[slot][:, None]
        out = jnp.where(valid[:, :, None, None, None], out, 0.0)
        attended = out.reshape(rows, HEADS * HD).astype(jnp.bfloat16)
        mixed = jnp.dot(attended, wo, preferred_element_type=jnp.float32)
        stream = lax.dynamic_slice_in_dim(residual, start, rows, 0).astype(jnp.float32)
        return (mixed + stream).astype(jnp.bfloat16)

    result = lax.map(one_slot, jnp.arange(count, dtype=jnp.int32))
    return result.reshape(count * rows, D)
```

```python
import functools

import jax
import jax.numpy as jnp
from jax import lax
from jax.experimental import pallas as pl
from jax.experimental.pallas import tpu as pltpu
from jax.sharding import PartitionSpec as P

HD = 128
RESP = 5
TL = 8
GROUPS = ((0, 1), (1, 1), (2, 1), (3, 1), (4, 1))
TN = 512
MESH = pl.DeviceIdType.MESH
LOG2E = 1.4426950408889634
NEG = -1e30


class Dims:
    def __init__(self, ndp, ntensor, pdev, plen, heads, width):
        self.ndp = ndp
        self.ntensor = ntensor
        self.ny = ntensor // 2
        self.pdev = pdev
        self.plen = plen
        self.heads = heads
        self.width = width
        self.tiles = width // TN
        self.half = self.tiles // 2
        self.rows = RESP * heads * TL
        self.qwidth = heads * HD


def bulk_wait(ref, sem):
    pltpu.make_async_copy(ref, ref, sem).wait()


def kernel(dims, refs_layout, *refs):
    names = dict(zip(refs_layout, refs, strict=True))
    idx, rlen, q_ref, own_ref = (names[k] for k in ("idx", "rlen", "q", "own"))
    kv_hbm, wo_hbm, res_hbm, out_ref = (names[k] for k in ("kv_hbm", "wo_hbm", "res_hbm", "out"))
    qv, kv, wo, res, fin = (names[k] for k in ("qv", "kv", "wo", "res", "fin"))
    orr, lser, ob, st_t, att = (names[k] for k in ("orr", "lser", "ob", "st_t", "att"))
    load_sem, z_sem, core_sem, ring_sem = (names[k] for k in ("load_sem", "z_sem", "core_sem", "ring_sem"))
    ndp, ny, pdev, heads = dims.ndp, dims.ny, dims.pdev, dims.heads
    tiles, half = dims.tiles, dims.half
    seg = heads * TL
    f32, bf16 = jnp.float32, jnp.bfloat16
    me = lax.axis_index("dp")
    tensor = lax.axis_index("tensor")
    ypos, core = tensor // 2, lax.rem(tensor, 2)
    partner = ypos * 2 + 1 - core
    y_next = lax.rem(ypos + 1, ny) * 2 + core
    y_prev = lax.rem(ypos + ny - 1, ny) * 2 + core
    o_from, o_home, o_qidx, o_back = 0, pdev, 2 * pdev, 2 * pdev + ndp
    o_plen = 2 * pdev + 2 * ndp
    cc = HD ** (-0.5) * LOG2E

    loads = [pltpu.make_async_copy(kv_hbm, kv, load_sem.at[0]), pltpu.make_async_copy(res_hbm, res, load_sem.at[1])]
    loads += [
        pltpu.make_async_copy(wo_hbm.at[:, pl.ds(n * TN, TN)], wo.at[n], load_sem.at[2 + n]) for n in range(tiles)
    ]
    for load in loads:
        load.start()

    barrier = pltpu.get_barrier_semaphore()

    def greet(k, carry):
        pl.semaphore_signal(barrier, inc=1, device_id=(lax.rem(me + k, ndp), tensor), device_id_type=MESH)
        return carry

    lax.fori_loop(1, ndp, greet, 0)
    for other in (partner, y_next, y_prev):
        pl.semaphore_signal(barrier, inc=1, device_id=(me, other), device_id_type=MESH)

    def turn(i, carry):
        x = q_ref[pl.ds(pl.multiple_of(i * 2 * RESP * TL, 2 * RESP * TL), 2 * RESP * TL), :].astype(f32)
        for part in range(2):
            pieces = [
                x[(part * RESP + r) * TL : (part * RESP + r + 1) * TL, h * HD : (h + 1) * HD]
                for r in range(RESP)
                for h in range(heads)
            ]
            qv[i * 2 + part] = jnp.concatenate(pieces, axis=0).astype(bf16)
        return carry

    lax.fori_loop(0, pdev // 2, turn, 0)
    pl.semaphore_wait(barrier, ndp - 1 + 3)

    def q_send(g):
        r0, size = GROUPS[g]
        qs, qr = names["qs", g], names["qr", g]
        span = pl.ds(r0 * seg, size * seg)

        def fill(h, carry):
            qs[h] = qv[idx[o_qidx + h], span, :]
            return carry

        lax.fori_loop(0, ndp, fill, 0)

        def send(k, carry):
            target = lax.rem(me + k, ndp)
            pltpu.make_async_remote_copy(
                src_ref=qs.at[target], dst_ref=qr.at[me], send_sem=z_sem.at[g, 0], recv_sem=z_sem.at[g, 1],
                device_id=(target, tensor), device_id_type=MESH,
            ).start()
            return carry

        lax.fori_loop(1, ndp, send, 0)
        qr[me] = qs[me]

    def own_part():
        n = 2 * dims.rows
        cols = 2 * RESP * TL
        row = lax.broadcasted_iota(jnp.int32, (n, cols), 0)
        col = lax.broadcasted_iota(jnp.int32, (n, cols), 1)
        seg_bits = (seg - 1).bit_length()
        seen = ((row >> seg_bits) == (col >> 3)) & ((col & 7) <= (row & 7))
        lane = lax.broadcasted_iota(jnp.int32, (dims.rows, 128), 1)

        def one(i, stat):
            x = own_ref[pl.ds(pl.multiple_of(i * cols, cols), cols), :]
            qp = jnp.concatenate([qv[i * 2], qv[i * 2 + 1]], axis=0)
            s = lax.dot_general(qp, x[:, :HD], (((1,), (1,)), ((), ())), preferred_element_type=f32)
            s = jnp.where(seen, s * cc, NEG)
            m = jnp.max(s, axis=1, keepdims=True)
            p = jnp.exp2(s - m)
            l = jnp.sum(p, axis=1, keepdims=True)
            o = jnp.dot(p.astype(bf16), x[:, HD:], preferred_element_type=f32) / l
            lse = m + jnp.log2(l)
            for part in range(2):
                cut = slice(part * dims.rows, (part + 1) * dims.rows)
                orr[i * 2 + part] = o[cut]
                stat = jnp.where(lane == i * 2 + part, lse[cut], stat)
            return stat

        lser[...] = lax.fori_loop(0, pdev // 2, one, jnp.zeros((dims.rows, 128), f32))

    def attend(g):
        size = GROUPS[g][1]
        n = size * seg
        qr = names["qr", g]
        bulk_wait(qr.at[pl.ds(0, ndp - 1)], z_sem.at[g, 1])
        col = lax.broadcasted_iota(jnp.int32, (n, dims.plen), 1)
        lane = lax.broadcasted_iota(jnp.int32, (n, 128), 1)

        def one(j, stat):
            qj = qr[idx[o_from + j]]
            s = lax.dot_general(qj, kv[j, :, :HD], (((1,), (1,)), ((), ())), preferred_element_type=f32)
            s = jnp.where(col < idx[o_plen + j], s * cc, NEG)
            m = jnp.max(s, axis=1, keepdims=True)
            p = jnp.exp2(s - m)
            l = jnp.sum(p, axis=1, keepdims=True)
            o = jnp.dot(p.astype(bf16), kv[j, :, HD:], preferred_element_type=f32) / l
            ob[j, pl.ds(0, n), :] = o.astype(bf16)
            return jnp.where(lane == j, m + jnp.log2(l), stat)

        stat = lax.fori_loop(0, pdev, one, jnp.zeros((n, 128), f32))
        for b in range(-(-n // 128)):
            block = stat[b * 128 : (b + 1) * 128]
            if block.shape[0] < 128:
                block = jnp.concatenate([block, jnp.zeros((128 - block.shape[0], 128), f32)], axis=0)
            st_t[:, pl.ds(b * 128, 128)] = jnp.transpose(block)[:pdev]

    def a_send(g):
        n = GROUPS[g][1] * seg
        as_, ar, ss, sr = (names[k, g] for k in ("as", "ar", "ss", "sr"))
        lanes = ss.shape[2]

        def fill(s, carry):
            j = idx[o_back + s]
            as_[s] = ob[j, pl.ds(0, n), :]
            ss[s] = st_t[pl.ds(j, 1), pl.ds(0, lanes)]
            return carry

        lax.fori_loop(0, ndp, fill, 0)

        def send(k, carry):
            target = lax.rem(me + k, ndp)
            for src, dst, at in ((as_, ar, 2), (ss, sr, 4)):
                pltpu.make_async_remote_copy(
                    src_ref=src.at[target], dst_ref=dst.at[me], send_sem=z_sem.at[g, at],
                    recv_sem=z_sem.at[g, at + 1], device_id=(target, tensor), device_id_type=MESH,
                ).start()
            return carry

        lax.fori_loop(1, ndp, send, 0)
        ar[me] = as_[me]
        sr[me] = ss[me]

    def merge(g):
        r0, size = GROUPS[g]
        n = size * seg
        ar, sr = names["ar", g], names["sr", g]
        bulk_wait(ar.at[pl.ds(0, ndp - 1)], z_sem.at[g, 3])
        bulk_wait(sr.at[pl.ds(0, ndp - 1)], z_sem.at[g, 5])
        homes = [idx[o_home + i] for i in range(pdev)]
        stat = jnp.concatenate([sr[homes[i]] for i in range(pdev)], axis=0)
        blocks = []
        for b in range(-(-n // 128)):
            block = jnp.concatenate([stat[:, b * 128 : (b + 1) * 128], jnp.zeros((128 - pdev, 128), f32)], axis=0)
            blocks.append(jnp.transpose(block))
        lp = jnp.concatenate(blocks, axis=0)[:n] if len(blocks) > 1 else blocks[0][:n]
        lr = lser[pl.ds(r0 * seg, n), :]
        w = 1.0 / (1.0 + jnp.exp2(lr - lp))
        position = lax.broadcasted_iota(jnp.int32, (seg, HD), 0) & 7
        for i in range(0, pdev, 2):
            pieces = [[], []]
            for part in range(2):
                wi = w[:, i + part : i + part + 1]
                op = ar[homes[i + part]].astype(f32)
                both = wi * op + (1.0 - wi) * orr[i + part, pl.ds(r0 * seg, n), :]
                for r in range(size):
                    x = both[r * seg : (r + 1) * seg]
                    x = jnp.where(position < rlen[i + part, r0 + r], x, 0.0)
                    x = jnp.concatenate([x[h * TL : (h + 1) * TL] for h in range(heads)], axis=1)
                    pieces[part].append(x)
            rows = [pieces[part][r] for r in range(size) for part in range(2)]
            owner = i // 2
            att[lax.rem(owner + core, 2), owner // 2, pl.ds(0, 2 * TL * size), :] = jnp.concatenate(rows, axis=0).astype(bf16)

    def project(g):
        size = GROUPS[g][1]
        n = 2 * TL * size
        cs, cr, po = (names[k, g] for k in ("cs", "cr", "po"))
        a = att[:, :, pl.ds(0, n), :].reshape(2 * ny * n, dims.qwidth)

        def tile(i, carry):
            x = jnp.dot(a, wo[i], preferred_element_type=f32).astype(bf16)
            cs[i] = x[ny * n :].reshape(ny, n, TN)
            pltpu.make_async_remote_copy(
                src_ref=cs.at[i], dst_ref=cr.at[i], send_sem=core_sem.at[g, 0], recv_sem=core_sem.at[g, 1],
                device_id=(me, partner), device_id_type=MESH,
            ).start()
            po[i] = x[: ny * n].reshape(ny, n, TN)
            return carry

        lax.fori_loop(0, tiles, tile, 0)

    def ring_copy(g, step, way):
        rs, rr = names["rs", g], names["rr", g]
        return pltpu.make_async_remote_copy(
            src_ref=rs.at[way, step], dst_ref=rr.at[way, step], send_sem=ring_sem.at[g, way, step, 0],
            recv_sem=ring_sem.at[g, way, step, 1], device_id=(me, y_next if way == 0 else y_prev), device_id_type=MESH,
        )

    def ring(g, step):
        cr, po, rs, rr = (names[k, g] for k in ("cr", "po", "rs", "rr"))
        if step == 0:
            bulk_wait(cr, core_sem.at[g, 1])
        for way in range(2):
            if step > 0:
                ring_copy(g, step - 1, way).wait_recv()
            chunk = lax.rem(ypos + ny - 1 - step, ny) if way == 0 else lax.rem(ypos + 1 + step, ny)

            def tile(i, carry):
                n = way * half + i
                x = po[n, chunk].astype(f32) + cr[n, chunk].astype(f32)
                if step > 0:
                    x = x + rr[way, step - 1, i].astype(f32)
                rs[way, step, i] = x.astype(bf16)
                return carry

            lax.fori_loop(0, half, tile, 0)
            ring_copy(g, step, way).start()

    def finish(g):
        r0, size = GROUPS[g]
        cr, po, rr = (names[k, g] for k in ("cr", "po", "rr"))
        for way in range(2):
            ring_copy(g, ny - 2, way).wait_recv()

            def tile(i, carry):
                n = way * half + i
                x = po[n, ypos].astype(f32) + cr[n, ypos].astype(f32) + rr[way, ny - 2, i].astype(f32)
                at = pl.ds(pl.multiple_of(n * TN, TN), TN)
                for r in range(size):
                    for part in range(2):
                        down = pl.ds(part * RESP * TL + (r0 + r) * TL, TL)
                        fin[down, at] = fin[down, at] + x[(r * 2 + part) * TL : (r * 2 + part + 1) * TL]
                return carry

            lax.fori_loop(0, half, tile, 0)

    def columns(body):
        def tile(n, carry):
            body(pl.ds(pl.multiple_of(n * TN, TN), TN))
            return carry

        lax.fori_loop(0, tiles, tile, 0)

    def start_total(at):
        fin[:, at] = res[:, at].astype(f32)

    def end_total(at):
        out_ref[:, at] = fin[:, at].astype(bf16)

    ng = len(GROUPS)
    q_send(0)
    if ng > 1:
        q_send(1)
    own_part()
    loads[1].wait()
    columns(start_total)
    loads[0].wait()
    for slot in range(ng + 3):
        if slot < ng:
            attend(slot)
            a_send(slot)
            if slot + 2 < ng:
                q_send(slot + 2)
        if 0 <= slot - 3 < ng:
            finish(slot - 3)
        if 0 <= slot - 2 < ng:
            ring(slot - 2, 1)
        if 0 <= slot - 1 < ng:
            merge(slot - 1)
            if slot == 1:
                for load in loads[2:]:
                    load.wait()
            project(slot - 1)
        if 0 <= slot - 2 < ng:
            ring(slot - 2, 2)
        if 0 <= slot - 1 < ng:
            ring(slot - 1, 0)
    columns(end_total)

    for g in range(ng):
        bulk_wait(names["qs", g].at[pl.ds(0, ndp - 1)], z_sem.at[g, 0])
        bulk_wait(names["as", g].at[pl.ds(0, ndp - 1)], z_sem.at[g, 2])
        bulk_wait(names["ss", g].at[pl.ds(0, ndp - 1)], z_sem.at[g, 4])
        bulk_wait(names["cs", g], core_sem.at[g, 0])
        for step in range(ny - 1):
            for way in range(2):
                ring_copy(g, step, way).wait_send()


def per_device(queries, resp_kv, prompt_kv, prompt_len, resp_len, dest, wo, residual):
    ndp, ntensor = lax.axis_size("dp"), lax.axis_size("tensor")
    me = lax.axis_index("dp")
    pdev, plen, _ = prompt_kv.shape
    heads = queries.shape[1] // HD
    width = wo.shape[1]
    total = dest.shape[0]
    dims = Dims(ndp, ntensor, pdev, plen, heads, width)
    ny, tiles, half = dims.ny, dims.tiles, dims.half
    seg = heads * TL

    slots = me * pdev + jnp.arange(pdev, dtype=jnp.int32)
    every = jnp.arange(total, dtype=jnp.int32)
    home = jnp.sum(jnp.where(dest[None, :] == slots[:, None], every[None, :], 0), axis=1) // pdev
    scorer = lax.dynamic_slice(dest, (me * pdev,), (pdev,)) // pdev
    live = lax.dynamic_slice(prompt_len, (me * pdev,), (pdev,))
    here = jnp.arange(pdev, dtype=jnp.int32)
    devices = jnp.arange(ndp, dtype=jnp.int32)
    qidx = jnp.sum(jnp.where(home[None, :] == devices[:, None], here[None, :], 0), axis=1)
    back = jnp.sum(jnp.where(scorer[None, :] == devices[:, None], here[None, :], 0), axis=1)
    idx = jnp.concatenate([scorer, home, qidx, back, live]).astype(jnp.int32)

    bf16, f32 = jnp.bfloat16, jnp.float32
    layout = ["idx", "rlen", "q", "own", "kv_hbm", "wo_hbm", "res_hbm", "out"]
    scratch = []

    def add(name, shape):
        layout.append(name)
        scratch.append(shape)

    add("qv", pltpu.VMEM((pdev, dims.rows, HD), bf16))
    add("kv", pltpu.VMEM(prompt_kv.shape, bf16))
    add("wo", pltpu.VMEM((tiles, wo.shape[0], TN), bf16))
    add("res", pltpu.VMEM(residual.shape, bf16))
    add("fin", pltpu.VMEM(residual.shape, f32))
    add("orr", pltpu.VMEM((pdev, dims.rows, HD), f32))
    add("lser", pltpu.VMEM((dims.rows, 128), f32))
    most = max(size for _, size in GROUPS)
    add("ob", pltpu.VMEM((pdev, most * seg, HD), bf16))
    add("st_t", pltpu.VMEM((pdev, -(-most * seg // 128) * 128), f32))
    add("att", pltpu.VMEM((2, ny, most * 2 * TL, dims.qwidth), bf16))
    for g, (_, size) in enumerate(GROUPS):
        n = size * seg
        for name in ("qs", "qr", "as", "ar"):
            add((name, g), pltpu.VMEM((ndp, n, HD), bf16))
        for name in ("ss", "sr"):
            add((name, g), pltpu.VMEM((ndp, 1, -(-n // 128) * 128), f32))
        for name in ("cs", "cr", "po"):
            add((name, g), pltpu.VMEM((tiles, ny, 2 * TL * size, TN), bf16))
        for name in ("rs", "rr"):
            add((name, g), pltpu.VMEM((2, ny - 1, half, 2 * TL * size, TN), bf16))
    ng = len(GROUPS)
    add("load_sem", pltpu.SemaphoreType.DMA((2 + tiles,)))
    add("z_sem", pltpu.SemaphoreType.DMA((ng, 6)))
    add("core_sem", pltpu.SemaphoreType.DMA((ng, 2)))
    add("ring_sem", pltpu.SemaphoreType.DMA((ng, 2, ny - 1, 2)))

    smem = pl.BlockSpec(memory_space=pltpu.SMEM)
    vmem = pl.BlockSpec(memory_space=pltpu.VMEM)
    hbm = pl.BlockSpec(memory_space=pl.ANY)
    return pl.pallas_call(
        functools.partial(kernel, dims, layout),
        out_shape=jax.ShapeDtypeStruct(residual.shape, bf16),
        in_specs=[smem, smem, vmem, vmem, hbm, hbm, hbm],
        out_specs=vmem,
        scratch_shapes=scratch,
        compiler_params=pltpu.CompilerParams(
            collective_id=0, has_side_effects=True, vmem_limit_bytes=60 * 2**20
        ),
    )(idx, resp_len, queries, resp_kv, prompt_kv, wo, residual)


def solution(mesh):
    in_specs = (
        P("dp", "tensor"),
        P("dp", "tensor"),
        P("dp", None, "tensor"),
        P(),
        P("dp", None),
        P(),
        P("tensor", None),
        P(("dp", "tensor"), None),
    )
    out_specs = P(("dp", "tensor"), None)
    return jax.shard_map(
        per_device, mesh=mesh, in_specs=in_specs, out_specs=out_specs, check_vma=False
    )
```

```python
import functools

import jax
import jax.numpy as jnp
from jax import lax
from jax.experimental import pallas as pl
from jax.experimental.pallas import tpu as pltpu
from jax.sharding import PartitionSpec as P

HD = 128
RESP = 5
TL = 8
GROUPS = ((0, 1), (1, 1), (2, 1), (3, 1), (4, 1))
TN = 512
SCOPES = False
ATT_UNROLL = 4
PROJ_UNROLL = 4
MESH = pl.DeviceIdType.MESH
LOG2E = 1.4426950408889634
NEG = -1e30


class Dims:
    def __init__(self, ndp, ntensor, pdev, plen, heads, width):
        self.ndp = ndp
        self.ntensor = ntensor
        self.ny = ntensor // 2
        self.pdev = pdev
        self.plen = plen
        self.heads = heads
        self.width = width
        self.tiles = width // TN
        self.half = self.tiles // 2
        self.rows = RESP * heads * TL
        self.qwidth = heads * HD


def bulk_wait(ref, sem):
    pltpu.make_async_copy(ref, ref, sem).wait()


def kernel(dims, refs_layout, *refs):
    names = dict(zip(refs_layout, refs, strict=True))
    idx, rlen, q_ref, own_ref = (names[k] for k in ("idx", "rlen", "q", "own"))
    dest, live = names["dest"], names["live"]
    kv_hbm, wo_hbm, res_hbm, out_ref = (names[k] for k in ("kv_hbm", "wo_hbm", "res_hbm", "out"))
    qv, kv, kt, wo, res, fin = (names[k] for k in ("qv", "kv", "kt", "wo", "res", "fin"))
    orr, lser, ob, st_t, att = (names[k] for k in ("orr", "lser", "ob", "st_t", "att"))
    load_sem, z_sem, core_sem, ring_sem = (names[k] for k in ("load_sem", "z_sem", "core_sem", "ring_sem"))
    ndp, ny, pdev, heads = dims.ndp, dims.ny, dims.pdev, dims.heads
    tiles, half = dims.tiles, dims.half
    seg = heads * TL
    f32, bf16 = jnp.float32, jnp.bfloat16
    me = lax.axis_index("dp")
    tensor = lax.axis_index("tensor")
    ypos, core = tensor // 2, lax.rem(tensor, 2)
    partner = ypos * 2 + 1 - core
    y_next = lax.rem(ypos + 1, ny) * 2 + core
    y_prev = lax.rem(ypos + ny - 1, ny) * 2 + core
    o_home, o_qidx, o_back = 0, pdev, pdev + ndp
    cc = HD ** (-0.5) * LOG2E

    loads = [pltpu.make_async_copy(kv_hbm, kv, load_sem.at[0]), pltpu.make_async_copy(res_hbm, res, load_sem.at[1])]
    loads += [
        pltpu.make_async_copy(wo_hbm.at[:, pl.ds(n * TN, TN)], wo.at[n], load_sem.at[2 + n]) for n in range(tiles)
    ]
    for load in loads:
        load.start()

    barrier = pltpu.get_barrier_semaphore()

    def greet(k, carry):
        pl.semaphore_signal(barrier, inc=1, device_id=(lax.rem(me + k, ndp), tensor), device_id_type=MESH)
        return carry

    lax.fori_loop(1, ndp, greet, 0)
    for other in (partner, y_next, y_prev):
        pl.semaphore_signal(barrier, inc=1, device_id=(me, other), device_id_type=MESH)

    def turn(i, carry):
        x = q_ref[pl.ds(pl.multiple_of(i * 2 * RESP * TL, 2 * RESP * TL), 2 * RESP * TL), :].astype(f32)
        for part in range(2):
            pieces = [
                x[(part * RESP + r) * TL : (part * RESP + r + 1) * TL, h * HD : (h + 1) * HD]
                for r in range(RESP)
                for h in range(heads)
            ]
            qv[i * 2 + part] = jnp.concatenate(pieces, axis=0).astype(bf16)
        return carry

    lax.fori_loop(0, pdev // 2, turn, 0)

    def all_here():
        pl.semaphore_wait(barrier, ndp - 1 + 3)

    def q_send(g):
        r0, size = GROUPS[g]
        qs, qr = names["qs", g], names["qr", g]
        span = pl.ds(r0 * seg, size * seg)

        def fill(h, carry):
            qs[h] = qv[idx[o_qidx + h], span, :]
            return carry

        lax.fori_loop(0, ndp, fill, 0)

        def send(k, carry):
            target = lax.rem(me + k, ndp)
            pltpu.make_async_remote_copy(
                src_ref=qs.at[target], dst_ref=qr.at[me], send_sem=z_sem.at[g, 0], recv_sem=z_sem.at[g, 1],
                device_id=(target, tensor), device_id_type=MESH,
            ).start()
            return carry

        lax.fori_loop(1, ndp, send, 0)
        qr[me] = qs[me]

    def turn_keys():
        loads[0].wait()

        def one(j, carry):
            kt[j] = jnp.transpose(kv[j, :, :HD])
            return carry

        lax.fori_loop(0, pdev, one, 0, unroll=2)

    def own_part():
        n = 2 * dims.rows
        cols = 2 * RESP * TL
        row = lax.broadcasted_iota(jnp.int32, (n, cols), 0)
        col = lax.broadcasted_iota(jnp.int32, (n, cols), 1)
        seg_bits = (seg - 1).bit_length()
        seen = ((row >> seg_bits) == (col >> 3)) & ((col & 7) <= (row & 7))
        lane = lax.broadcasted_iota(jnp.int32, (dims.rows, 128), 1)

        def one(i, stat):
            x = own_ref[pl.ds(pl.multiple_of(i * cols, cols), cols), :]
            qp = jnp.concatenate([qv[i * 2], qv[i * 2 + 1]], axis=0)
            s = lax.dot_general(qp, x[:, :HD], (((1,), (1,)), ((), ())), preferred_element_type=f32)
            s = jnp.where(seen, s * cc, NEG)
            m = jnp.max(s, axis=1, keepdims=True)
            p = jnp.exp2(s - m)
            l = jnp.sum(p, axis=1, keepdims=True)
            o = jnp.dot(p.astype(bf16), x[:, HD:], preferred_element_type=f32) / l
            lse = m + jnp.log2(l)
            for part in range(2):
                cut = slice(part * dims.rows, (part + 1) * dims.rows)
                orr[i * 2 + part] = o[cut]
                stat = jnp.where(lane == i * 2 + part, lse[cut], stat)
            return stat

        lser[...] = lax.fori_loop(0, pdev // 2, one, jnp.zeros((dims.rows, 128), f32))

    def q_wait(g):
        bulk_wait(names["qr", g].at[pl.ds(0, ndp - 1)], z_sem.at[g, 1])

    def attend(g):
        size = GROUPS[g][1]
        n = size * seg
        qr = names["qr", g]
        col = lax.broadcasted_iota(jnp.int32, (n, dims.plen), 1)
        lane = lax.broadcasted_iota(jnp.int32, (n, 128), 1)

        def one(j, stat):
            qj = qr[dest[me * pdev + j] // pdev]
            s = jnp.dot(qj, kt[j], preferred_element_type=f32)
            s = jnp.where(col < live[me * pdev + j], s * cc, NEG)
            m = jnp.max(s, axis=1, keepdims=True)
            p = jnp.exp2(s - m)
            l = jnp.sum(p, axis=1, keepdims=True)
            o = jnp.dot(p.astype(bf16), kv[j, :, HD:], preferred_element_type=f32) / l
            ob[j, pl.ds(0, n), :] = o.astype(bf16)
            return jnp.where(lane == j, m + jnp.log2(l), stat)

        stat = lax.fori_loop(0, pdev, one, jnp.zeros((n, 128), f32), unroll=ATT_UNROLL)
        for b in range(-(-n // 128)):
            block = stat[b * 128 : (b + 1) * 128]
            if block.shape[0] < 128:
                block = jnp.concatenate([block, jnp.zeros((128 - block.shape[0], 128), f32)], axis=0)
            st_t[:, pl.ds(b * 128, 128)] = jnp.transpose(block)[:pdev]

    def a_send(g):
        n = GROUPS[g][1] * seg
        as_, ar, ss, sr = (names[k, g] for k in ("as", "ar", "ss", "sr"))
        lanes = ss.shape[2]

        def fill(s, carry):
            j = idx[o_back + s]
            as_[s] = ob[j, pl.ds(0, n), :]
            ss[s] = st_t[pl.ds(j, 1), pl.ds(0, lanes)]
            return carry

        lax.fori_loop(0, ndp, fill, 0)

        def send(k, carry):
            target = lax.rem(me + k, ndp)
            for src, dst, at in ((as_, ar, 2), (ss, sr, 4)):
                pltpu.make_async_remote_copy(
                    src_ref=src.at[target], dst_ref=dst.at[me], send_sem=z_sem.at[g, at],
                    recv_sem=z_sem.at[g, at + 1], device_id=(target, tensor), device_id_type=MESH,
                ).start()
            return carry

        lax.fori_loop(1, ndp, send, 0)
        ar[me] = as_[me]
        sr[me] = ss[me]

    def a_wait(g):
        bulk_wait(names["ar", g].at[pl.ds(0, ndp - 1)], z_sem.at[g, 3])
        bulk_wait(names["sr", g].at[pl.ds(0, ndp - 1)], z_sem.at[g, 5])

    def merge(g):
        r0, size = GROUPS[g]
        n = size * seg
        ar, sr = names["ar", g], names["sr", g]
        homes = [idx[o_home + i] for i in range(pdev)]
        stat = jnp.concatenate([sr[homes[i]] for i in range(pdev)], axis=0)
        blocks = []
        for b in range(-(-n // 128)):
            block = jnp.concatenate([stat[:, b * 128 : (b + 1) * 128], jnp.zeros((128 - pdev, 128), f32)], axis=0)
            blocks.append(jnp.transpose(block))
        lp = jnp.concatenate(blocks, axis=0)[:n] if len(blocks) > 1 else blocks[0][:n]
        lr = lser[pl.ds(r0 * seg, n), :]
        w = 1.0 / (1.0 + jnp.exp2(lr - lp))
        position = lax.broadcasted_iota(jnp.int32, (seg, HD), 0) & 7
        for i in range(0, pdev, 2):
            pieces = [[], []]
            for part in range(2):
                wi = w[:, i + part : i + part + 1]
                op = ar[homes[i + part]].astype(f32)
                both = wi * op + (1.0 - wi) * orr[i + part, pl.ds(r0 * seg, n), :]
                for r in range(size):
                    x = both[r * seg : (r + 1) * seg]
                    x = jnp.where(position < rlen[r0 + r, i + part], x, 0.0)
                    x = jnp.concatenate([x[h * TL : (h + 1) * TL] for h in range(heads)], axis=1)
                    pieces[part].append(x)
            rows = [pieces[part][r] for r in range(size) for part in range(2)]
            owner = i // 2
            att[lax.rem(owner + core, 2), owner // 2, pl.ds(0, 2 * TL * size), :] = jnp.concatenate(rows, axis=0).astype(bf16)

    def project(g, way):
        size = GROUPS[g][1]
        n = 2 * TL * size
        cs, cr, po = (names[k, g] for k in ("cs", "cr", "po"))
        a = att[:, :, pl.ds(0, n), :].reshape(2 * ny * n, dims.qwidth)

        def tile(i, carry):
            x = jnp.dot(a, wo[i], preferred_element_type=f32).astype(bf16)
            cs[i] = x[ny * n :].reshape(ny, n, TN)
            pltpu.make_async_remote_copy(
                src_ref=cs.at[i], dst_ref=cr.at[i], send_sem=core_sem.at[g, way, 0], recv_sem=core_sem.at[g, way, 1],
                device_id=(me, partner), device_id_type=MESH,
            ).start()
            po[i] = x[: ny * n].reshape(ny, n, TN)
            return carry

        lax.fori_loop(way * half, (way + 1) * half, tile, 0, unroll=PROJ_UNROLL)

    def core_wait(g, way):
        bulk_wait(names["cr", g].at[pl.ds(way * half, half)], core_sem.at[g, way, 1])

    def across(y, way):
        return y + 1 - 2 * lax.rem(y, 2) if way == 0 else ny - 1 - y

    def y_copy(g, step, way):
        send, recv = (names[k, g] for k in (("xs", "xr"), ("ws", "wr"))[step])
        other = across(ypos, way if step == 0 else 1 - way) * 2 + core
        return pltpu.make_async_remote_copy(
            src_ref=send.at[way], dst_ref=recv.at[way], send_sem=ring_sem.at[g, way, step, 0],
            recv_sem=ring_sem.at[g, way, step, 1], device_id=(me, other), device_id_type=MESH,
        )

    def both_cores(g, n, owner):
        return names["po", g][n, owner].astype(f32) + names["cr", g][n, owner].astype(f32)

    def y_first(g, way):
        xs = names["xs", g]
        other = across(ypos, way)
        owners = (other, across(other, 1 - way))

        def tile(i, carry):
            for k in range(2):
                xs[way, k, i] = both_cores(g, way * half + i, owners[k]).astype(bf16)
            return carry

        lax.fori_loop(0, half, tile, 0, unroll=2)
        y_copy(g, 0, way).start()

    def y_wait(g, step, way):
        y_copy(g, step, way).wait_recv()

    def y_second(g, way):
        xr, ws = names["xr", g], names["ws", g]
        owner = across(ypos, 1 - way)

        def tile(i, carry):
            ws[way, i] = (both_cores(g, way * half + i, owner) + xr[way, 1, i].astype(f32)).astype(bf16)
            return carry

        lax.fori_loop(0, half, tile, 0, unroll=2)
        y_copy(g, 1, way).start()

    def finish(g, way):
        r0, size = GROUPS[g]
        xr, wr = names["xr", g], names["wr", g]

        def tile(i, carry):
            n = way * half + i
            x = both_cores(g, n, ypos) + xr[way, 0, i].astype(f32) + wr[way, i].astype(f32)
            at = pl.ds(pl.multiple_of(n * TN, TN), TN)
            for r in range(size):
                for part in range(2):
                    down = pl.ds(part * RESP * TL + (r0 + r) * TL, TL)
                    fin[down, at] = fin[down, at] + x[(r * 2 + part) * TL : (r * 2 + part + 1) * TL]
            return carry

        lax.fori_loop(0, half, tile, 0, unroll=2)

    def columns(body):
        def tile(n, carry):
            body(pl.ds(pl.multiple_of(n * TN, TN), TN))
            return carry

        lax.fori_loop(0, tiles, tile, 0)

    def start_total(at):
        fin[:, at] = res[:, at].astype(f32)

    def end_total(at):
        out_ref[:, at] = fin[:, at].astype(bf16)

    ng = len(GROUPS)

    def loaded():
        for load in loads[2:]:
            load.wait()

    def total_of_residual():
        loads[1].wait()
        columns(start_total)

    def run(step, *args):
        if SCOPES:
            with jax.named_scope("_".join([step.__name__, *map(str, args)])):
                step(*args)
        else:
            step(*args)

    run(all_here)
    run(q_send, 0)
    if ng > 1:
        run(q_send, 1)
    run(turn_keys)
    run(own_part)
    run(total_of_residual)
    for slot in range(ng + 2):
        if slot < ng:
            run(q_wait, slot)
            run(attend, slot)
            run(a_send, slot)
            if slot + 2 < ng:
                run(q_send, slot + 2)
        if 0 <= slot - 3:
            for way in range(2):
                run(y_wait, slot - 3, 1, way)
                run(finish, slot - 3, way)
        if 0 <= slot - 1 < ng:
            run(a_wait, slot - 1)
            run(merge, slot - 1)
            if slot == 1:
                run(loaded)
            run(project, slot - 1, 0)
            run(project, slot - 1, 1)
        if 0 <= slot - 2:
            for way in range(2):
                run(y_wait, slot - 2, 0, way)
                run(y_second, slot - 2, way)
        if 0 <= slot - 1 < ng:
            for way in range(2):
                run(core_wait, slot - 1, way)
                run(y_first, slot - 1, way)
    for way in range(2):
        run(y_wait, ng - 1, 1, way)
        run(finish, ng - 1, way)
    columns(end_total)

    for g in range(ng):
        bulk_wait(names["qs", g].at[pl.ds(0, ndp - 1)], z_sem.at[g, 0])
        bulk_wait(names["as", g].at[pl.ds(0, ndp - 1)], z_sem.at[g, 2])
        bulk_wait(names["ss", g].at[pl.ds(0, ndp - 1)], z_sem.at[g, 4])
        for way in range(2):
            bulk_wait(names["cs", g].at[pl.ds(way * half, half)], core_sem.at[g, way, 0])
            for step in range(2):
                y_copy(g, step, way).wait_send()


def per_device(queries, resp_kv, prompt_kv, prompt_len, resp_len, dest, wo, residual):
    ndp, ntensor = lax.axis_size("dp"), lax.axis_size("tensor")
    me = lax.axis_index("dp")
    pdev, plen, _ = prompt_kv.shape
    heads = queries.shape[1] // HD
    width = wo.shape[1]
    total = dest.shape[0]
    dims = Dims(ndp, ntensor, pdev, plen, heads, width)
    ny, tiles, half = dims.ny, dims.tiles, dims.half
    seg = heads * TL

    k = lax.broadcasted_iota(jnp.int32, (pdev + 2 * ndp, total), 0)
    p = lax.broadcasted_iota(jnp.int32, (pdev + 2 * ndp, total), 1)
    d = jnp.broadcast_to(dest[None, :], k.shape)
    first, second = k < pdev, k < pdev + ndp
    theirs = jnp.where(second, d, p) // pdev == me
    same = jnp.where(first, d % pdev == k, jnp.where(second, p // pdev == k - pdev, d // pdev == k - pdev - ndp))
    value = jnp.where(first, p // pdev, jnp.where(second, d, p) % pdev)
    idx = jnp.sum(jnp.where(theirs & same, value, 0), axis=1)

    bf16, f32 = jnp.bfloat16, jnp.float32
    layout = ["idx", "dest", "live", "rlen", "q", "own", "kv_hbm", "wo_hbm", "res_hbm", "out"]
    scratch = []

    def add(name, shape):
        layout.append(name)
        scratch.append(shape)

    add("qv", pltpu.VMEM((pdev, dims.rows, HD), bf16))
    add("kv", pltpu.VMEM(prompt_kv.shape, bf16))
    add("kt", pltpu.VMEM((pdev, HD, plen), bf16))
    add("wo", pltpu.VMEM((tiles, wo.shape[0], TN), bf16))
    add("res", pltpu.VMEM(residual.shape, bf16))
    add("fin", pltpu.VMEM(residual.shape, f32))
    add("orr", pltpu.VMEM((pdev, dims.rows, HD), f32))
    add("lser", pltpu.VMEM((dims.rows, 128), f32))
    most = max(size for _, size in GROUPS)
    add("ob", pltpu.VMEM((pdev, most * seg, HD), bf16))
    add("st_t", pltpu.VMEM((pdev, -(-most * seg // 128) * 128), f32))
    add("att", pltpu.VMEM((2, ny, most * 2 * TL, dims.qwidth), bf16))
    for g, (_, size) in enumerate(GROUPS):
        n = size * seg
        for name in ("qs", "qr", "as", "ar"):
            add((name, g), pltpu.VMEM((ndp, n, HD), bf16))
        for name in ("ss", "sr"):
            add((name, g), pltpu.VMEM((ndp, 1, -(-n // 128) * 128), f32))
        for name in ("cs", "cr", "po"):
            add((name, g), pltpu.VMEM((tiles, ny, 2 * TL * size, TN), bf16))
        for name in ("xs", "xr"):
            add((name, g), pltpu.VMEM((2, 2, half, 2 * TL * size, TN), bf16))
        for name in ("ws", "wr"):
            add((name, g), pltpu.VMEM((2, half, 2 * TL * size, TN), bf16))
    ng = len(GROUPS)
    add("load_sem", pltpu.SemaphoreType.DMA((2 + tiles,)))
    add("z_sem", pltpu.SemaphoreType.DMA((ng, 6)))
    add("core_sem", pltpu.SemaphoreType.DMA((ng, 2, 2)))
    add("ring_sem", pltpu.SemaphoreType.DMA((ng, 2, 2, 2)))

    smem = pl.BlockSpec(memory_space=pltpu.SMEM)
    vmem = pl.BlockSpec(memory_space=pltpu.VMEM)
    hbm = pl.BlockSpec(memory_space=pl.ANY)
    return pl.pallas_call(
        functools.partial(kernel, dims, layout),
        out_shape=jax.ShapeDtypeStruct(residual.shape, bf16),
        in_specs=[smem, smem, smem, smem, vmem, vmem, hbm, hbm, hbm],
        out_specs=vmem,
        scratch_shapes=scratch,
        compiler_params=pltpu.CompilerParams(
            collective_id=0, has_side_effects=True, vmem_limit_bytes=60 * 2**20
        ),
    )(idx, dest, prompt_len, resp_len.T, queries, resp_kv, prompt_kv, wo, residual)


def solution(mesh):
    in_specs = (
        P("dp", "tensor"),
        P("dp", "tensor"),
        P("dp", None, "tensor"),
        P(),
        P("dp", None),
        P(),
        P("tensor", None),
        P(("dp", "tensor"), None),
    )
    out_specs = P(("dp", "tensor"), None)
    return jax.shard_map(
        per_device, mesh=mesh, in_specs=in_specs, out_specs=out_specs, check_vma=False
    )
```

```python
import functools

import jax
import jax.numpy as jnp
from jax import lax
from jax.experimental import pallas as pl
from jax.experimental.pallas import tpu as pltpu
from jax.sharding import PartitionSpec as P

HD = 128
RESP = 5
TL = 8
GROUPS = ((0, 1), (1, 1), (2, 1), (3, 1), (4, 1))
TN = 512
AHEAD = 2
ATT_UNROLL = 4
PROJ_UNROLL = 4
MESH = pl.DeviceIdType.MESH
LOG2E = 1.4426950408889634
NEG = -1e30


class Dims:
    def __init__(self, ndp, ntensor, pdev, plen, heads, width):
        self.ndp = ndp
        self.ntensor = ntensor
        self.ny = ntensor // 2
        self.pdev = pdev
        self.plen = plen
        self.heads = heads
        self.width = width
        self.tiles = width // TN
        self.half = self.tiles // 2
        self.rows = RESP * heads * TL
        self.qwidth = heads * HD


def bulk_wait(ref, sem):
    pltpu.make_async_copy(ref, ref, sem).wait()


def kernel(dims, refs_layout, *refs):
    names = dict(zip(refs_layout, refs, strict=True))
    idx, rlen, q_ref, own_ref = (names[k] for k in ("idx", "rlen", "q", "own"))
    dest, live = names["dest"], names["live"]
    kv_hbm, wo_hbm, res_hbm, out_ref = (names[k] for k in ("kv_hbm", "wo_hbm", "res_hbm", "out"))
    qv, kv, kt, vo, wo, res, fin = (names[k] for k in ("qv", "kv", "kt", "vo", "wo", "res", "fin"))
    orr, lser, ob, st_t, att = (names[k] for k in ("orr", "lser", "ob", "st_t", "att"))
    load_sem, z_sem, core_sem, ring_sem = (names[k] for k in ("load_sem", "z_sem", "core_sem", "ring_sem"))
    ndp, ny, pdev, heads = dims.ndp, dims.ny, dims.pdev, dims.heads
    tiles, half = dims.tiles, dims.half
    seg = heads * TL
    f32, bf16 = jnp.float32, jnp.bfloat16
    me = lax.axis_index("dp")
    tensor = lax.axis_index("tensor")
    ypos, core = tensor // 2, lax.rem(tensor, 2)
    partner = ypos * 2 + 1 - core
    y_next = lax.rem(ypos + 1, ny) * 2 + core
    y_prev = lax.rem(ypos + ny - 1, ny) * 2 + core
    o_home, o_qidx, o_back = 0, pdev, pdev + ndp
    cc = HD ** (-0.5) * LOG2E

    loads = [pltpu.make_async_copy(kv_hbm, kv, load_sem.at[0]), pltpu.make_async_copy(res_hbm, res, load_sem.at[1])]
    loads += [
        pltpu.make_async_copy(wo_hbm.at[:, pl.ds(n * TN, TN)], wo.at[n], load_sem.at[2 + n]) for n in range(tiles)
    ]
    for load in loads:
        load.start()

    barrier = pltpu.get_barrier_semaphore()

    def greet(k, carry):
        pl.semaphore_signal(barrier, inc=1, device_id=(lax.rem(me + k, ndp), tensor), device_id_type=MESH)
        return carry

    lax.fori_loop(1, ndp, greet, 0)
    for other in (partner, y_next, y_prev):
        pl.semaphore_signal(barrier, inc=1, device_id=(me, other), device_id_type=MESH)

    def turn(i, carry):
        x = q_ref[pl.ds(pl.multiple_of(i * 2 * RESP * TL, 2 * RESP * TL), 2 * RESP * TL), :].astype(f32)
        for part in range(2):
            pieces = [
                x[(part * RESP + r) * TL : (part * RESP + r + 1) * TL, h * HD : (h + 1) * HD]
                for r in range(RESP)
                for h in range(heads)
            ]
            qv[i * 2 + part] = jnp.concatenate(pieces, axis=0).astype(bf16)
        return carry

    lax.fori_loop(0, pdev // 2, turn, 0)

    def all_here():
        pl.semaphore_wait(barrier, ndp - 1 + 3)

    def q_send(g):
        r0, size = GROUPS[g]
        qs, qr = names["qs", g], names["qr", g]
        span = pl.ds(r0 * seg, size * seg)

        def fill(h, carry):
            qs[h] = qv[idx[o_qidx + h], span, :]
            return carry

        lax.fori_loop(0, ndp, fill, 0)

        def send(k, carry):
            target = lax.rem(me + k, ndp)
            pltpu.make_async_remote_copy(
                src_ref=qs.at[target], dst_ref=qr.at[me], send_sem=z_sem.at[g, 0], recv_sem=z_sem.at[g, 1],
                device_id=(target, tensor), device_id_type=MESH,
            ).start()
            return carry

        lax.fori_loop(1, ndp, send, 0)
        qr[me] = qs[me]

    def turn_keys():
        loads[0].wait()

        def one(j, carry):
            kt[j] = jnp.transpose(kv[j, :, :HD])
            vo[j, :, :HD] = jnp.ones((dims.plen, HD), bf16)
            vo[j, :, HD:] = kv[j, :, HD:]
            return carry

        lax.fori_loop(0, pdev, one, 0, unroll=2)

    def own_part():
        n = 2 * dims.rows
        cols = 2 * RESP * TL
        row = lax.broadcasted_iota(jnp.int32, (n, cols), 0)
        col = lax.broadcasted_iota(jnp.int32, (n, cols), 1)
        seg_bits = (seg - 1).bit_length()
        seen = ((row >> seg_bits) == (col >> 3)) & ((col & 7) <= (row & 7))
        lane = lax.broadcasted_iota(jnp.int32, (dims.rows, 128), 1)

        def one(i, stat):
            x = own_ref[pl.ds(pl.multiple_of(i * cols, cols), cols), :]
            qp = jnp.concatenate([qv[i * 2], qv[i * 2 + 1]], axis=0)
            s = lax.dot_general(qp, x[:, :HD], (((1,), (1,)), ((), ())), preferred_element_type=f32)
            s = jnp.where(seen, s * cc, NEG)
            m = jnp.max(s, axis=1, keepdims=True)
            p = jnp.exp2(s - m)
            l = jnp.sum(p, axis=1, keepdims=True)
            o = jnp.dot(p.astype(bf16), x[:, HD:], preferred_element_type=f32) / l
            lse = m + jnp.log2(l)
            for part in range(2):
                cut = slice(part * dims.rows, (part + 1) * dims.rows)
                orr[i * 2 + part] = o[cut]
                stat = jnp.where(lane == i * 2 + part, lse[cut], stat)
            return stat

        lser[...] = lax.fori_loop(0, pdev // 2, one, jnp.zeros((dims.rows, 128), f32))

    def q_wait(g):
        bulk_wait(names["qr", g].at[pl.ds(0, ndp - 1)], z_sem.at[g, 1])

    def attend(g):
        size = GROUPS[g][1]
        n = size * seg
        qr = names["qr", g]
        col = lax.broadcasted_iota(jnp.int32, (n, dims.plen), 1)
        lane = lax.broadcasted_iota(jnp.int32, (n, 128), 1)

        def one(j, stat):
            qj = qr[dest[me * pdev + j] // pdev]
            s = jnp.dot(qj, kt[j], preferred_element_type=f32)
            s = jnp.where(col < live[me * pdev + j], s * cc, NEG)
            m = jnp.max(s, axis=1, keepdims=True)
            p = jnp.exp2(s - m).astype(bf16)
            both = jnp.dot(p, vo[j], preferred_element_type=f32)
            l, o = both[:, :HD], both[:, HD:]
            o = o / l
            ob[j, pl.ds(0, n), :] = o.astype(bf16)
            return jnp.where(lane == j, m + jnp.log2(l), stat)

        stat = lax.fori_loop(0, pdev, one, jnp.zeros((n, 128), f32), unroll=ATT_UNROLL)
        for b in range(-(-n // 128)):
            block = stat[b * 128 : (b + 1) * 128]
            if block.shape[0] < 128:
                block = jnp.concatenate([block, jnp.zeros((128 - block.shape[0], 128), f32)], axis=0)
            st_t[:, pl.ds(b * 128, 128)] = jnp.transpose(block)[:pdev]

    def a_send(g):
        n = GROUPS[g][1] * seg
        as_, ar, ss, sr = (names[k, g] for k in ("as", "ar", "ss", "sr"))
        lanes = ss.shape[2]

        def fill(s, carry):
            j = idx[o_back + s]
            as_[s] = ob[j, pl.ds(0, n), :]
            ss[s] = st_t[pl.ds(j, 1), pl.ds(0, lanes)]
            return carry

        lax.fori_loop(0, ndp, fill, 0)

        def send(k, carry):
            target = lax.rem(me + k, ndp)
            for src, dst, at in ((as_, ar, 2), (ss, sr, 4)):
                pltpu.make_async_remote_copy(
                    src_ref=src.at[target], dst_ref=dst.at[me], send_sem=z_sem.at[g, at],
                    recv_sem=z_sem.at[g, at + 1], device_id=(target, tensor), device_id_type=MESH,
                ).start()
            return carry

        lax.fori_loop(1, ndp, send, 0)
        ar[me] = as_[me]
        sr[me] = ss[me]

    def a_wait(g):
        bulk_wait(names["ar", g].at[pl.ds(0, ndp - 1)], z_sem.at[g, 3])
        bulk_wait(names["sr", g].at[pl.ds(0, ndp - 1)], z_sem.at[g, 5])

    def merge(g):
        r0, size = GROUPS[g]
        n = size * seg
        ar, sr = names["ar", g], names["sr", g]
        homes = [idx[o_home + i] for i in range(pdev)]
        stat = jnp.concatenate([sr[homes[i]] for i in range(pdev)], axis=0)
        blocks = []
        for b in range(-(-n // 128)):
            block = jnp.concatenate([stat[:, b * 128 : (b + 1) * 128], jnp.zeros((128 - pdev, 128), f32)], axis=0)
            blocks.append(jnp.transpose(block))
        lp = jnp.concatenate(blocks, axis=0)[:n] if len(blocks) > 1 else blocks[0][:n]
        lr = lser[pl.ds(r0 * seg, n), :]
        w = 1.0 / (1.0 + jnp.exp2(lr - lp))
        position = lax.broadcasted_iota(jnp.int32, (seg, HD), 0) & 7
        for i in range(0, pdev, 2):
            pieces = [[], []]
            for part in range(2):
                wi = w[:, i + part : i + part + 1]
                op = ar[homes[i + part]].astype(f32)
                both = wi * op + (1.0 - wi) * orr[i + part, pl.ds(r0 * seg, n), :]
                for r in range(size):
                    x = both[r * seg : (r + 1) * seg]
                    x = jnp.where(position < rlen[r0 + r, i + part], x, 0.0)
                    x = jnp.concatenate([x[h * TL : (h + 1) * TL] for h in range(heads)], axis=1)
                    pieces[part].append(x)
            rows = [pieces[part][r] for r in range(size) for part in range(2)]
            owner = i // 2
            att[lax.rem(owner + core, 2), owner // 2, pl.ds(0, 2 * TL * size), :] = jnp.concatenate(rows, axis=0).astype(bf16)

    def project(g, way):
        size = GROUPS[g][1]
        n = 2 * TL * size
        cs, cr, po = (names[k, g] for k in ("cs", "cr", "po"))
        a = att[:, :, pl.ds(0, n), :].reshape(2 * ny * n, dims.qwidth)

        def tile(i, carry):
            x = jnp.dot(a, wo[i], preferred_element_type=f32).astype(bf16)
            cs[i] = x[ny * n :].reshape(ny, n, TN)
            pltpu.make_async_remote_copy(
                src_ref=cs.at[i], dst_ref=cr.at[i], send_sem=core_sem.at[g, way, 0], recv_sem=core_sem.at[g, way, 1],
                device_id=(me, partner), device_id_type=MESH,
            ).start()
            po[i] = x[: ny * n].reshape(ny, n, TN)
            return carry

        lax.fori_loop(way * half, (way + 1) * half, tile, 0, unroll=PROJ_UNROLL)

    def core_wait(g, way):
        bulk_wait(names["cr", g].at[pl.ds(way * half, half)], core_sem.at[g, way, 1])

    def across(y, way):
        return y + 1 - 2 * lax.rem(y, 2) if way == 0 else ny - 1 - y

    def y_copy(g, step, way):
        send, recv = (names[k, g] for k in (("xs", "xr"), ("ws", "wr"))[step])
        other = across(ypos, way if step == 0 else 1 - way) * 2 + core
        return pltpu.make_async_remote_copy(
            src_ref=send.at[way], dst_ref=recv.at[way], send_sem=ring_sem.at[g, way, step, 0],
            recv_sem=ring_sem.at[g, way, step, 1], device_id=(me, other), device_id_type=MESH,
        )

    def both_cores(g, n, owner):
        return names["po", g][n, owner].astype(f32) + names["cr", g][n, owner].astype(f32)

    def y_first(g, way):
        xs = names["xs", g]
        other = across(ypos, way)
        owners = (other, across(other, 1 - way))

        def tile(i, carry):
            for k in range(2):
                xs[way, k, i] = both_cores(g, way * half + i, owners[k]).astype(bf16)
            return carry

        lax.fori_loop(0, half, tile, 0, unroll=2)
        y_copy(g, 0, way).start()

    def y_wait(g, step, way):
        y_copy(g, step, way).wait_recv()

    def y_second(g, way):
        xr, ws = names["xr", g], names["ws", g]
        owner = across(ypos, 1 - way)

        def tile(i, carry):
            ws[way, i] = (both_cores(g, way * half + i, owner) + xr[way, 1, i].astype(f32)).astype(bf16)
            return carry

        lax.fori_loop(0, half, tile, 0, unroll=2)
        y_copy(g, 1, way).start()

    def finish(g, way):
        r0, size = GROUPS[g]
        xr, wr = names["xr", g], names["wr", g]

        def tile(i, carry):
            n = way * half + i
            x = both_cores(g, n, ypos) + xr[way, 0, i].astype(f32) + wr[way, i].astype(f32)
            at = pl.ds(pl.multiple_of(n * TN, TN), TN)
            for r in range(size):
                for part in range(2):
                    down = pl.ds(part * RESP * TL + (r0 + r) * TL, TL)
                    fin[down, at] = fin[down, at] + x[(r * 2 + part) * TL : (r * 2 + part + 1) * TL]
            return carry

        lax.fori_loop(0, half, tile, 0, unroll=2)

    def q_sent(g):
        bulk_wait(names["qs", g].at[pl.ds(0, ndp - 1)], z_sem.at[g, 0])

    def a_sent(g):
        bulk_wait(names["as", g].at[pl.ds(0, ndp - 1)], z_sem.at[g, 2])
        bulk_wait(names["ss", g].at[pl.ds(0, ndp - 1)], z_sem.at[g, 4])

    def core_sent(g, way):
        bulk_wait(names["cs", g].at[pl.ds(way * half, half)], core_sem.at[g, way, 0])

    def y_sent(g, step, way):
        y_copy(g, step, way).wait_send()

    def columns(body):
        def tile(n, carry):
            body(pl.ds(pl.multiple_of(n * TN, TN), TN))
            return carry

        lax.fori_loop(0, tiles, tile, 0)

    def start_total(at):
        fin[:, at] = res[:, at].astype(f32)

    def end_total(at):
        out_ref[:, at] = fin[:, at].astype(bf16)

    ng = len(GROUPS)

    def loaded():
        for load in loads[2:]:
            load.wait()

    def total_of_residual():
        loads[1].wait()
        columns(start_total)

    def run(step, *args):
        step(*args)

    run(all_here)
    for g in range(min(AHEAD, ng)):
        run(q_send, g)
    run(turn_keys)
    run(own_part)
    run(total_of_residual)
    for slot in range(ng + 2):
        if slot < ng:
            run(q_wait, slot)
            run(attend, slot)
            run(a_send, slot)
            if slot + AHEAD < ng:
                run(q_send, slot + AHEAD)
        if 0 <= slot - 1 < ng:
            run(a_wait, slot - 1)
            run(merge, slot - 1)
            if slot == 1:
                run(loaded)
            run(project, slot - 1, 0)
            run(project, slot - 1, 1)
            for way in range(2):
                run(core_wait, slot - 1, way)
                run(y_first, slot - 1, way)
        if 0 <= slot - 2:
            for way in range(2):
                run(y_wait, slot - 2, 0, way)
                run(y_second, slot - 2, way)
        if 0 <= slot - 3:
            for way in range(2):
                run(y_wait, slot - 3, 1, way)
                run(finish, slot - 3, way)
    for way in range(2):
        run(y_wait, ng - 1, 1, way)
        run(finish, ng - 1, way)
    columns(end_total)

    for g in range(ng):
        run(q_sent, g)
        run(a_sent, g)
        for way in range(2):
            run(core_sent, g, way)
            run(y_sent, g, 0, way)
            run(y_sent, g, 1, way)


def per_device(queries, resp_kv, prompt_kv, prompt_len, resp_len, dest, wo, residual):
    ndp, ntensor = lax.axis_size("dp"), lax.axis_size("tensor")
    me = lax.axis_index("dp")
    pdev, plen, _ = prompt_kv.shape
    heads = queries.shape[1] // HD
    width = wo.shape[1]
    total = dest.shape[0]
    dims = Dims(ndp, ntensor, pdev, plen, heads, width)
    ny, tiles, half = dims.ny, dims.tiles, dims.half
    seg = heads * TL

    k = lax.broadcasted_iota(jnp.int32, (pdev + 2 * ndp, total), 0)
    p = lax.broadcasted_iota(jnp.int32, (pdev + 2 * ndp, total), 1)
    d = jnp.broadcast_to(dest[None, :], k.shape)
    first, second = k < pdev, k < pdev + ndp
    theirs = jnp.where(second, d, p) // pdev == me
    same = jnp.where(first, d % pdev == k, jnp.where(second, p // pdev == k - pdev, d // pdev == k - pdev - ndp))
    value = jnp.where(first, p // pdev, jnp.where(second, d, p) % pdev)
    idx = jnp.sum(jnp.where(theirs & same, value, 0), axis=1)

    bf16, f32 = jnp.bfloat16, jnp.float32
    layout = ["idx", "dest", "live", "rlen", "q", "own", "kv_hbm", "wo_hbm", "res_hbm", "out"]
    scratch = []

    def add(name, shape):
        layout.append(name)
        scratch.append(shape)

    add("qv", pltpu.VMEM((pdev, dims.rows, HD), bf16))
    add("kv", pltpu.VMEM(prompt_kv.shape, bf16))
    add("kt", pltpu.VMEM((pdev, HD, plen), bf16))
    add("vo", pltpu.VMEM((pdev, plen, 2 * HD), bf16))
    add("wo", pltpu.VMEM((tiles, wo.shape[0], TN), bf16))
    add("res", pltpu.VMEM(residual.shape, bf16))
    add("fin", pltpu.VMEM(residual.shape, f32))
    add("orr", pltpu.VMEM((pdev, dims.rows, HD), f32))
    add("lser", pltpu.VMEM((dims.rows, 128), f32))
    most = max(size for _, size in GROUPS)
    add("ob", pltpu.VMEM((pdev, most * seg, HD), bf16))
    add("st_t", pltpu.VMEM((pdev, -(-most * seg // 128) * 128), f32))
    add("att", pltpu.VMEM((2, ny, most * 2 * TL, dims.qwidth), bf16))
    for g, (_, size) in enumerate(GROUPS):
        n = size * seg
        for name in ("qs", "qr", "as", "ar"):
            add((name, g), pltpu.VMEM((ndp, n, HD), bf16))
        for name in ("ss", "sr"):
            add((name, g), pltpu.VMEM((ndp, 1, -(-n // 128) * 128), f32))
        for name in ("cs", "cr", "po"):
            add((name, g), pltpu.VMEM((tiles, ny, 2 * TL * size, TN), bf16))
        for name in ("xs", "xr"):
            add((name, g), pltpu.VMEM((2, 2, half, 2 * TL * size, TN), bf16))
        for name in ("ws", "wr"):
            add((name, g), pltpu.VMEM((2, half, 2 * TL * size, TN), bf16))
    ng = len(GROUPS)
    add("load_sem", pltpu.SemaphoreType.DMA((2 + tiles,)))
    add("z_sem", pltpu.SemaphoreType.DMA((ng, 6)))
    add("core_sem", pltpu.SemaphoreType.DMA((ng, 2, 2)))
    add("ring_sem", pltpu.SemaphoreType.DMA((ng, 2, 2, 2)))

    smem = pl.BlockSpec(memory_space=pltpu.SMEM)
    vmem = pl.BlockSpec(memory_space=pltpu.VMEM)
    hbm = pl.BlockSpec(memory_space=pl.ANY)
    return pl.pallas_call(
        functools.partial(kernel, dims, layout),
        out_shape=jax.ShapeDtypeStruct(residual.shape, bf16),
        in_specs=[smem, smem, smem, smem, vmem, vmem, hbm, hbm, hbm],
        out_specs=vmem,
        scratch_shapes=scratch,
        compiler_params=pltpu.CompilerParams(
            collective_id=0, has_side_effects=True, vmem_limit_bytes=60 * 2**20
        ),
    )(idx, dest, prompt_len, resp_len.T, queries, resp_kv, prompt_kv, wo, residual)


def solution(mesh):
    in_specs = (
        P("dp", "tensor"),
        P("dp", "tensor"),
        P("dp", None, "tensor"),
        P(),
        P("dp", None),
        P(),
        P("tensor", None),
        P(("dp", "tensor"), None),
    )
    out_specs = P(("dp", "tensor"), None)
    return jax.shard_map(
        per_device, mesh=mesh, in_specs=in_specs, out_specs=out_specs, check_vma=False
    )
```

```python
import functools

import jax
import jax.numpy as jnp
import numpy as np
from jax import lax
from jax.experimental import pallas as pl
from jax.experimental.pallas import tpu as pltpu
from jax.sharding import PartitionSpec as P

HD = 128
RESP = 5
TL = 8
GROUPS = ((0, 1), (1, 1), (2, 1), (3, 1), (4, 1))
TN = 512
AHEAD = 2
ATT_UNROLL = 8
PROJ_UNROLL = 4
MESH = pl.DeviceIdType.MESH
LOG2E = 1.4426950408889634
NEG = -1e30


class Dims:
    def __init__(self, ndp, ntensor, pdev, plen, heads, width):
        self.ndp = ndp
        self.ntensor = ntensor
        self.ny = ntensor // 2
        self.pdev = pdev
        self.plen = plen
        self.heads = heads
        self.width = width
        self.tiles = width // TN
        self.half = self.tiles // 2
        self.rows = RESP * heads * TL
        self.qwidth = heads * HD


def bulk_wait(ref, sem):
    pltpu.make_async_copy(ref, ref, sem).wait()


def kernel(dims, refs_layout, *refs):
    names = dict(zip(refs_layout, refs, strict=True))
    idx, rlen, q_ref, own_ref = (names[k] for k in ("idx", "rlen", "q", "own"))
    dest, live = names["dest"], names["live"]
    kv_hbm, wo_hbm, res_hbm, out_ref = (names[k] for k in ("kv_hbm", "wo_hbm", "res_hbm", "out"))
    qv, kv, kt, vo, wo, res, fin = (names[k] for k in ("qv", "kv", "kt", "vo", "wo", "res", "fin"))
    orr, lser, ob, st_t, att = (names[k] for k in ("orr", "lser", "ob", "st_t", "att"))
    load_sem, z_sem, core_sem, ring_sem = (names[k] for k in ("load_sem", "z_sem", "core_sem", "ring_sem"))
    ndp, ny, pdev, heads = dims.ndp, dims.ny, dims.pdev, dims.heads
    tiles, half = dims.tiles, dims.half
    seg = heads * TL
    f32, bf16 = jnp.float32, jnp.bfloat16
    me = lax.axis_index("dp")
    tensor = lax.axis_index("tensor")
    ypos, core = tensor // 2, lax.rem(tensor, 2)
    partner = ypos * 2 + 1 - core
    y_next = lax.rem(ypos + 1, ny) * 2 + core
    y_prev = lax.rem(ypos + ny - 1, ny) * 2 + core
    o_home, o_qidx, o_back = 0, pdev, pdev + ndp
    cc = HD ** (-0.5) * LOG2E

    loads = [pltpu.make_async_copy(kv_hbm, kv, load_sem.at[0]), pltpu.make_async_copy(res_hbm, res, load_sem.at[1])]
    loads += [
        pltpu.make_async_copy(wo_hbm.at[:, pl.ds(n * TN, TN)], wo.at[n], load_sem.at[2 + n]) for n in range(tiles)
    ]
    for load in loads:
        load.start()

    barrier = pltpu.get_barrier_semaphore()

    def greet(k, carry):
        pl.semaphore_signal(barrier, inc=1, device_id=(lax.rem(me + k, ndp), tensor), device_id_type=MESH)
        return carry

    lax.fori_loop(1, ndp, greet, 0)
    for other in (partner, y_next, y_prev):
        pl.semaphore_signal(barrier, inc=1, device_id=(me, other), device_id_type=MESH)

    def turn(i, carry):
        x = q_ref[pl.ds(pl.multiple_of(i * 2 * RESP * TL, 2 * RESP * TL), 2 * RESP * TL), :].astype(f32)
        for part in range(2):
            pieces = [
                x[(part * RESP + r) * TL : (part * RESP + r + 1) * TL, h * HD : (h + 1) * HD]
                for r in range(RESP)
                for h in range(heads)
            ]
            qv[i * 2 + part] = jnp.concatenate(pieces, axis=0).astype(bf16)
        return carry

    lax.fori_loop(0, pdev // 2, turn, 0)

    def all_here():
        pl.semaphore_wait(barrier, ndp - 1 + 3)

    def q_send(g):
        r0, size = GROUPS[g]
        qs, qr = names["qs", g], names["qr", g]
        span = pl.ds(r0 * seg, size * seg)

        def fill(h, carry):
            qs[h] = qv[idx[o_qidx + h], span, :]
            return carry

        lax.fori_loop(0, ndp, fill, 0)

        def send(k, carry):
            target = lax.rem(me + k, ndp)
            pltpu.make_async_remote_copy(
                src_ref=qs.at[target], dst_ref=qr.at[me], send_sem=z_sem.at[g, 0], recv_sem=z_sem.at[g, 1],
                device_id=(target, tensor), device_id_type=MESH,
            ).start()
            return carry

        lax.fori_loop(1, ndp, send, 0)
        qr[me] = qs[me]

    def turn_keys():
        loads[0].wait()

        def one(j, carry):
            kt[j] = jnp.transpose(kv[j, :, :HD])
            vo[j, :, :HD] = jnp.ones((dims.plen, HD), bf16)
            vo[j, :, HD:] = kv[j, :, HD:]
            return carry

        lax.fori_loop(0, pdev, one, 0, unroll=2)

    def own_part():
        n = 2 * dims.rows
        cols = 2 * RESP * TL
        row = lax.broadcasted_iota(jnp.int32, (n, cols), 0)
        col = lax.broadcasted_iota(jnp.int32, (n, cols), 1)
        seg_bits = (seg - 1).bit_length()
        seen = ((row >> seg_bits) == (col >> 3)) & ((col & 7) <= (row & 7))
        lane = lax.broadcasted_iota(jnp.int32, (dims.rows, 128), 1)

        def one(i, stat):
            x = own_ref[pl.ds(pl.multiple_of(i * cols, cols), cols), :]
            qp = jnp.concatenate([qv[i * 2], qv[i * 2 + 1]], axis=0)
            s = lax.dot_general(qp, x[:, :HD], (((1,), (1,)), ((), ())), preferred_element_type=f32)
            s = jnp.where(seen, s * cc, NEG)
            m = jnp.max(s, axis=1, keepdims=True)
            p = jnp.exp2(s - m)
            l = jnp.sum(p, axis=1, keepdims=True)
            o = jnp.dot(p.astype(bf16), x[:, HD:], preferred_element_type=f32) / l
            lse = m + jnp.log2(l)
            for part in range(2):
                cut = slice(part * dims.rows, (part + 1) * dims.rows)
                orr[i * 2 + part] = o[cut]
                stat = jnp.where(lane == i * 2 + part, lse[cut], stat)
            return stat

        lser[...] = lax.fori_loop(0, pdev // 2, one, jnp.zeros((dims.rows, 128), f32))

    def q_wait(g):
        bulk_wait(names["qr", g].at[pl.ds(0, ndp - 1)], z_sem.at[g, 1])

    def attend(g):
        size = GROUPS[g][1]
        n = size * seg
        qr = names["qr", g]
        col = lax.broadcasted_iota(jnp.int32, (n, dims.plen), 1)
        lane = lax.broadcasted_iota(jnp.int32, (n, 128), 1)

        def one(j, stat):
            qj = qr[dest[me * pdev + j] // pdev]
            s = jnp.dot(qj, kt[j], preferred_element_type=f32)
            s = jnp.where(col < live[me * pdev + j], s * cc, NEG)
            m = jnp.max(s, axis=1, keepdims=True)
            p = jnp.exp2(s - m).astype(bf16)
            both = jnp.dot(p, vo[j], preferred_element_type=f32)
            l, o = both[:, :HD], both[:, HD:]
            o = o / l
            ob[j, pl.ds(0, n), :] = o.astype(bf16)
            return jnp.where(lane == j, m + jnp.log2(l), stat)

        stat = lax.fori_loop(0, pdev, one, jnp.zeros((n, 128), f32), unroll=ATT_UNROLL)
        for b in range(-(-n // 128)):
            block = stat[b * 128 : (b + 1) * 128]
            if block.shape[0] < 128:
                block = jnp.concatenate([block, jnp.zeros((128 - block.shape[0], 128), f32)], axis=0)
            st_t[:, pl.ds(b * 128, 128)] = jnp.transpose(block)[:pdev]

    def a_send(g):
        n = GROUPS[g][1] * seg
        as_, ar, ss, sr = (names[k, g] for k in ("as", "ar", "ss", "sr"))
        lanes = ss.shape[2]

        def fill(s, carry):
            j = idx[o_back + s]
            as_[s] = ob[j, pl.ds(0, n), :]
            ss[s] = st_t[pl.ds(j, 1), pl.ds(0, lanes)]
            return carry

        lax.fori_loop(0, ndp, fill, 0)

        def send(k, carry):
            target = lax.rem(me + k, ndp)
            for src, dst, at in ((as_, ar, 2), (ss, sr, 4)):
                pltpu.make_async_remote_copy(
                    src_ref=src.at[target], dst_ref=dst.at[me], send_sem=z_sem.at[g, at],
                    recv_sem=z_sem.at[g, at + 1], device_id=(target, tensor), device_id_type=MESH,
                ).start()
            return carry

        lax.fori_loop(1, ndp, send, 0)
        ar[me] = as_[me]
        sr[me] = ss[me]

    def a_wait(g):
        bulk_wait(names["ar", g].at[pl.ds(0, ndp - 1)], z_sem.at[g, 3])
        bulk_wait(names["sr", g].at[pl.ds(0, ndp - 1)], z_sem.at[g, 5])

    def merge(g):
        r0, size = GROUPS[g]
        n = size * seg
        ar, sr = names["ar", g], names["sr", g]
        homes = [idx[o_home + i] for i in range(pdev)]
        stat = jnp.concatenate([sr[homes[i]] for i in range(pdev)], axis=0)
        blocks = []
        for b in range(-(-n // 128)):
            block = jnp.concatenate([stat[:, b * 128 : (b + 1) * 128], jnp.zeros((128 - pdev, 128), f32)], axis=0)
            blocks.append(jnp.transpose(block))
        lp = jnp.concatenate(blocks, axis=0)[:n] if len(blocks) > 1 else blocks[0][:n]
        lr = lser[pl.ds(r0 * seg, n), :]
        w = 1.0 / (1.0 + jnp.exp2(lr - lp))
        position = lax.broadcasted_iota(jnp.int32, (seg, HD), 0) & 7
        for i in range(0, pdev, 2):
            pieces = [[], []]
            for part in range(2):
                wi = w[:, i + part : i + part + 1]
                op = ar[homes[i + part]].astype(f32)
                both = wi * op + (1.0 - wi) * orr[i + part, pl.ds(r0 * seg, n), :]
                for r in range(size):
                    x = both[r * seg : (r + 1) * seg]
                    x = jnp.where(position < rlen[r0 + r, i + part], x, 0.0)
                    x = jnp.concatenate([x[h * TL : (h + 1) * TL] for h in range(heads)], axis=1)
                    pieces[part].append(x)
            rows = [pieces[part][r] for r in range(size) for part in range(2)]
            owner = i // 2
            att[lax.rem(owner + core, 2), owner // 2, pl.ds(0, 2 * TL * size), :] = jnp.concatenate(rows, axis=0).astype(bf16)

    def project(g, way):
        size = GROUPS[g][1]
        n = 2 * TL * size
        cs, cr, po = (names[k, g] for k in ("cs", "cr", "po"))
        a = att[:, :, pl.ds(0, n), :].reshape(2 * ny * n, dims.qwidth)

        def tile(i, carry):
            x = jnp.dot(a, wo[i], preferred_element_type=f32).astype(bf16)
            cs[i] = x[ny * n :].reshape(ny, n, TN)
            pltpu.make_async_remote_copy(
                src_ref=cs.at[i], dst_ref=cr.at[i], send_sem=core_sem.at[g, way, 0], recv_sem=core_sem.at[g, way, 1],
                device_id=(me, partner), device_id_type=MESH,
            ).start()
            po[i] = x[: ny * n].reshape(ny, n, TN)
            return carry

        lax.fori_loop(way * half, (way + 1) * half, tile, 0, unroll=PROJ_UNROLL)

    def core_wait(g, way):
        bulk_wait(names["cr", g].at[pl.ds(way * half, half)], core_sem.at[g, way, 1])

    def across(y, way):
        return y + 1 - 2 * lax.rem(y, 2) if way == 0 else ny - 1 - y

    def y_copy(g, step, way):
        send, recv = (names[k, g] for k in (("xs", "xr"), ("ws", "wr"))[step])
        other = across(ypos, way if step == 0 else 1 - way) * 2 + core
        return pltpu.make_async_remote_copy(
            src_ref=send.at[way], dst_ref=recv.at[way], send_sem=ring_sem.at[g, way, step, 0],
            recv_sem=ring_sem.at[g, way, step, 1], device_id=(me, other), device_id_type=MESH,
        )

    def both_cores(g, n, owner):
        return names["po", g][n, owner].astype(f32) + names["cr", g][n, owner].astype(f32)

    def y_first(g, way):
        xs = names["xs", g]
        other = across(ypos, way)
        owners = (other, across(other, 1 - way))

        def tile(i, carry):
            for k in range(2):
                xs[way, k, i] = both_cores(g, way * half + i, owners[k]).astype(bf16)
            return carry

        lax.fori_loop(0, half, tile, 0, unroll=2)
        y_copy(g, 0, way).start()

    def y_wait(g, step, way):
        y_copy(g, step, way).wait_recv()

    def y_second(g, way):
        xr, ws = names["xr", g], names["ws", g]
        owner = across(ypos, 1 - way)

        def tile(i, carry):
            ws[way, i] = (both_cores(g, way * half + i, owner) + xr[way, 1, i].astype(f32)).astype(bf16)
            return carry

        lax.fori_loop(0, half, tile, 0, unroll=2)
        y_copy(g, 1, way).start()

    def finish(g, way):
        r0, size = GROUPS[g]
        xr, wr = names["xr", g], names["wr", g]

        def tile(i, carry):
            n = way * half + i
            x = both_cores(g, n, ypos) + xr[way, 0, i].astype(f32) + wr[way, i].astype(f32)
            at = pl.ds(pl.multiple_of(n * TN, TN), TN)
            for r in range(size):
                for part in range(2):
                    down = pl.ds(part * RESP * TL + (r0 + r) * TL, TL)
                    fin[down, at] = fin[down, at] + x[(r * 2 + part) * TL : (r * 2 + part + 1) * TL]
            return carry

        lax.fori_loop(0, half, tile, 0, unroll=2)

    def q_sent(g):
        bulk_wait(names["qs", g].at[pl.ds(0, ndp - 1)], z_sem.at[g, 0])

    def a_sent(g):
        bulk_wait(names["as", g].at[pl.ds(0, ndp - 1)], z_sem.at[g, 2])
        bulk_wait(names["ss", g].at[pl.ds(0, ndp - 1)], z_sem.at[g, 4])

    def core_sent(g, way):
        bulk_wait(names["cs", g].at[pl.ds(way * half, half)], core_sem.at[g, way, 0])

    def y_sent(g, step, way):
        y_copy(g, step, way).wait_send()

    def columns(body):
        def tile(n, carry):
            body(pl.ds(pl.multiple_of(n * TN, TN), TN))
            return carry

        lax.fori_loop(0, tiles, tile, 0)

    def start_total(at):
        fin[:, at] = res[:, at].astype(f32)

    def end_total(at):
        out_ref[:, at] = fin[:, at].astype(bf16)

    ng = len(GROUPS)

    def loaded():
        for load in loads[2:]:
            load.wait()

    def total_of_residual():
        loads[1].wait()
        columns(start_total)

    def run(step, *args):
        step(*args)

    run(all_here)
    for g in range(min(AHEAD, ng)):
        run(q_send, g)
    run(turn_keys)
    run(own_part)
    run(total_of_residual)
    for slot in range(ng + 2):
        if slot < ng:
            run(q_wait, slot)
            run(attend, slot)
            run(a_send, slot)
            if slot + AHEAD < ng:
                run(q_send, slot + AHEAD)
        if 0 <= slot - 1 < ng:
            run(a_wait, slot - 1)
            run(merge, slot - 1)
            if slot == 1:
                run(loaded)
            run(project, slot - 1, 0)
            run(project, slot - 1, 1)
            for way in range(2):
                run(core_wait, slot - 1, way)
                run(y_first, slot - 1, way)
        if 0 <= slot - 2:
            for way in range(2):
                run(y_wait, slot - 2, 0, way)
                run(y_second, slot - 2, way)
        if 0 <= slot - 3:
            for way in range(2):
                run(y_wait, slot - 3, 1, way)
                run(finish, slot - 3, way)
    for way in range(2):
        run(y_wait, ng - 1, 1, way)
        run(finish, ng - 1, way)
    columns(end_total)

    for g in range(ng):
        run(q_sent, g)
        run(a_sent, g)
        for way in range(2):
            run(core_sent, g, way)
            run(y_sent, g, 0, way)
            run(y_sent, g, 1, way)


def per_device(queries, resp_kv, prompt_kv, prompt_len, resp_len, dest, wo, residual):
    ndp, ntensor = lax.axis_size("dp"), lax.axis_size("tensor")
    me = lax.axis_index("dp")
    pdev, plen, _ = prompt_kv.shape
    heads = queries.shape[1] // HD
    width = wo.shape[1]
    total = dest.shape[0]
    dims = Dims(ndp, ntensor, pdev, plen, heads, width)
    ny, tiles, half = dims.ny, dims.tiles, dims.half
    seg = heads * TL

    k = np.arange(pdev + 2 * ndp, dtype=np.int32)[:, None]
    p = np.arange(total, dtype=np.int32)[None, :]
    first, second = k < pdev, k < pdev + ndp
    asked = np.where(first, k, np.where(second, k - pdev, k - pdev - ndp)).astype(np.int32)
    p_dev, p_at = p // pdev, p % pdev
    bits = (pdev - 1).bit_length()
    d_dev, d_at = dest[None, :] >> bits, dest[None, :] & (pdev - 1)
    theirs = jnp.where(second, d_dev, p_dev) == me
    same = jnp.where(first, d_at, jnp.where(second, p_dev, d_dev)) == asked
    value = jnp.where(first, p_dev, jnp.where(second, d_at, p_at))
    idx = jnp.sum(jnp.where(theirs & same, value, 0), axis=1)

    bf16, f32 = jnp.bfloat16, jnp.float32
    layout = ["idx", "dest", "live", "rlen", "q", "own", "kv_hbm", "wo_hbm", "res_hbm", "out"]
    scratch = []

    def add(name, shape):
        layout.append(name)
        scratch.append(shape)

    add("qv", pltpu.VMEM((pdev, dims.rows, HD), bf16))
    add("kv", pltpu.VMEM(prompt_kv.shape, bf16))
    add("kt", pltpu.VMEM((pdev, HD, plen), bf16))
    add("vo", pltpu.VMEM((pdev, plen, 2 * HD), bf16))
    add("wo", pltpu.VMEM((tiles, wo.shape[0], TN), bf16))
    add("res", pltpu.VMEM(residual.shape, bf16))
    add("fin", pltpu.VMEM(residual.shape, f32))
    add("orr", pltpu.VMEM((pdev, dims.rows, HD), f32))
    add("lser", pltpu.VMEM((dims.rows, 128), f32))
    most = max(size for _, size in GROUPS)
    add("ob", pltpu.VMEM((pdev, most * seg, HD), bf16))
    add("st_t", pltpu.VMEM((pdev, -(-most * seg // 128) * 128), f32))
    add("att", pltpu.VMEM((2, ny, most * 2 * TL, dims.qwidth), bf16))
    for g, (_, size) in enumerate(GROUPS):
        n = size * seg
        for name in ("qs", "qr", "as", "ar"):
            add((name, g), pltpu.VMEM((ndp, n, HD), bf16))
        for name in ("ss", "sr"):
            add((name, g), pltpu.VMEM((ndp, 1, -(-n // 128) * 128), f32))
        for name in ("cs", "cr", "po"):
            add((name, g), pltpu.VMEM((tiles, ny, 2 * TL * size, TN), bf16))
        for name in ("xs", "xr"):
            add((name, g), pltpu.VMEM((2, 2, half, 2 * TL * size, TN), bf16))
        for name in ("ws", "wr"):
            add((name, g), pltpu.VMEM((2, half, 2 * TL * size, TN), bf16))
    ng = len(GROUPS)
    add("load_sem", pltpu.SemaphoreType.DMA((2 + tiles,)))
    add("z_sem", pltpu.SemaphoreType.DMA((ng, 6)))
    add("core_sem", pltpu.SemaphoreType.DMA((ng, 2, 2)))
    add("ring_sem", pltpu.SemaphoreType.DMA((ng, 2, 2, 2)))

    smem = pl.BlockSpec(memory_space=pltpu.SMEM)
    vmem = pl.BlockSpec(memory_space=pltpu.VMEM)
    hbm = pl.BlockSpec(memory_space=pl.ANY)
    return pl.pallas_call(
        functools.partial(kernel, dims, layout),
        out_shape=jax.ShapeDtypeStruct(residual.shape, bf16),
        in_specs=[smem, smem, smem, smem, vmem, vmem, hbm, hbm, hbm],
        out_specs=vmem,
        scratch_shapes=scratch,
        compiler_params=pltpu.CompilerParams(
            collective_id=0, has_side_effects=True, vmem_limit_bytes=60 * 2**20
        ),
    )(idx, dest, prompt_len, resp_len.T, queries, resp_kv, prompt_kv, wo, residual)


def solution(mesh):
    in_specs = (
        P("dp", "tensor"),
        P("dp", "tensor"),
        P("dp", None, "tensor"),
        P(),
        P("dp", None),
        P(),
        P("tensor", None),
        P(("dp", "tensor"), None),
    )
    out_specs = P(("dp", "tensor"), None)
    return jax.shard_map(
        per_device, mesh=mesh, in_specs=in_specs, out_specs=out_specs, check_vma=False
    )
```
